32 devices in a mesh: groups: 2 (over y), pool: 4 (over z), tp: 4 (over x, core).
Axes of the slice: x: 2, y: 2, z: 4, core: 2. Of those that a mesh axis runs over, the one named last changes fastest.
Arguments:
- span_q: bfloat16 [128, 32, 4096], P(('groups', 'pool'), None, 'tp'), parts along dimension 0, may hold values from -200 to 200
- span_kv: bfloat16 [128, 2, 32, 1024], P(('groups', 'pool'), None, None, 'tp'), parts along dimension 0, may hold values from -6 to 6
- span_offset: int32 [128], P(('groups', 'pool')), parts along dimension 0, may hold values from 0 to 2048, as said below
- span_length: int32 [128], P(('groups', 'pool')), parts along dimension 0, may hold values from 1 to 32, as said below
- span_dest: int32 [128], P(('groups', 'pool')), parts along dimension 0, may hold values from 0 to 3, as said below
- prefix_kv: bfloat16 [128, 2, 128, 1024], P(('groups', 'pool'), None, None, 'tp'), parts along dimension 0, may hold values from -6 to 6
- resident_kv: bfloat16 [64, 2, 512, 1024], P(('groups', 'pool'), None, None, 'tp'), parts along dimension 0, may hold values from -6 to 6
- seq_length: int32 [64], P(('groups', 'pool')), parts along dimension 0, may hold values from 1 to 512, as said below
- decode_q: bfloat16 [64, 4, 4096], P(('groups', 'pool'), None, 'tp'), parts along dimension 0, may hold values from -200 to 200
- decode_kv: bfloat16 [64, 2, 4, 1024], P(('groups', 'pool'), None, None, 'tp'), parts along dimension 0, may hold values from -6 to 6
- block_target: int32 [128], P(('groups', 'pool')), parts along dimension 0, may hold values from 0 to 31, as said below
Outputs:
- prefill_out: bfloat16 [128, 32, 4096], P(('groups', 'pool'), None, 'tp'), parts along dimension 0
- decode_out: bfloat16 [64, 4, 4096], P(('groups', 'pool'), None, 'tp'), parts along dimension 0
The draws below stay inside these ranges and needn't reach their ends.
There are 2 independent parts, one for each index of `groups`. The reference program is written for one: setup_inputs(seed, part) draws one part's arguments, and reference() takes and returns one part's arrays. A program takes and returns all parts, laid end to end along the dimension named above; each array names one. Nothing has to cross between parts.
Inputs may be any that keep to these rules, and one draw needn't show every extreme that they name: `span_dest`: the 16 spans of one device name at most 4 spans for any one instance; in every draw some instance gets exactly 4 spans from every device. `span_offset`: 2048 is reached in every draw. `span_length`: 32 is reached in every draw. `seq_length`: 512 is reached in every draw. `block_target`: sequence g belongs to owner g // 8. The 16 blocks of one device name at most 4 blocks for any one owner; in every draw some owner gets exactly 4 blocks from every device.
All inputs are finite; a program needn't handle non-finite values.
Results may differ from the reference program's by a relative error of at most 0.0045.
Values may be sent and summed in bfloat16 or wider, within the bound.
A program may use at most 64 MiB of HBM per device.

```python
import math
import jax
import jax.numpy as jnp
from jax import lax

HD = 128
KVH = 8
QPK = 4
QH = 32
SPAN = 32
CH_DEV = 16
CAP = 4
SPANS = 64
BLK = 128
PB = 16
PREF = 2048
NBLK = 64
MCAP = 4
SEQ_DEV = 8
SEQS = 32
RES = 512
STEPS = 4
N_POOL = 4


def spread_owners(key, holders, per_holder, capacity):
    busy_key, perm_key, order_key = jax.random.split(key, 3)
    busiest = jax.random.randint(busy_key, (), 0, holders)
    others = 1 + jax.vmap(lambda single: jax.random.permutation(single, holders - 1))(jax.random.split(perm_key, holders))
    ordinal = jnp.arange(per_holder)
    picked = jnp.maximum(ordinal - capacity, 0) % (holders - 1)
    rest = jnp.take(others, picked, axis=1)
    owners = jnp.where(ordinal[None, :] < capacity, busiest, (busiest + rest) % holders)
    shuffle = jax.vmap(lambda single: jax.random.permutation(single, per_holder))(jax.random.split(order_key, holders))
    owners = jnp.take_along_axis(owners, shuffle, axis=1)
    return owners.reshape(-1).astype(jnp.int32)


def lifted_rows(key, shape, peak):
    base_key, lift_key = jax.random.split(key)
    base = jax.random.normal(base_key, shape, jnp.float32)
    chance = jax.random.uniform(lift_key, shape[:-1] + (1,), jnp.float32)
    factor = 1.0 + (peak - 1.0) * (chance > 0.9).astype(jnp.float32)
    return jnp.clip(base * factor, -6.0, 6.0)


def reach_top(key, count, lowest, highest):
    value_key, spot_key = jax.random.split(key)
    values = jax.random.randint(value_key, (count,), lowest, highest + 1)
    spot = jax.random.randint(spot_key, (), 0, count)
    return jnp.where(jnp.arange(count) == spot, highest, values).astype(jnp.int32)


def draw_span_q(key, part):
    key = jax.random.fold_in(key, 21)
    return lifted_rows(key, (SPANS, SPAN, KVH * QPK * HD), 1.0).astype(jnp.bfloat16)


def draw_decode_q(key, part):
    key = jax.random.fold_in(key, 22)
    return lifted_rows(key, (SEQS, STEPS, KVH * QPK * HD), 1.0).astype(jnp.bfloat16)


def draw_span_offset(key, part):
    key = jax.random.fold_in(key, 31)
    return reach_top(key, SPANS, 0, PREF)


def draw_span_length(key, part):
    key = jax.random.fold_in(key, 32)
    return reach_top(key, SPANS, 1, SPAN)


def draw_seq_length(key, part):
    key = jax.random.fold_in(key, 33)
    return reach_top(key, SEQS, 1, RES)


def draw_span_dest(key, part):
    key = jax.random.fold_in(key, 41)
    return spread_owners(key, N_POOL, CH_DEV, CAP)


def draw_block_target(key, part):
    key = jax.random.fold_in(key, 42)
    owner_key, seat_key = jax.random.split(key)
    owners = spread_owners(owner_key, N_POOL, PB, MCAP)
    seats = jax.random.randint(seat_key, (NBLK,), 0, SEQ_DEV)
    return (owners * SEQ_DEV + seats).astype(jnp.int32)


def shard_levels(key, extent, shards, smallest, high):
    gain, own = 1.0, jax.random.fold_in(key, 6)
    for axis_at, parts in shards:
        steps = jnp.exp(jax.random.uniform(jax.random.fold_in(own, axis_at), (parts,), jnp.float32, smallest / len(shards), high / len(shards)))
        gain = gain * jnp.repeat(steps, extent[axis_at] // parts).reshape([-1 if axis == axis_at else 1 for axis in range(len(extent))])
    return gain


def bell_draw(stream_key, dims, deviation, most, shards=(), kind=jnp.bfloat16):
    level = shard_levels(stream_key, dims, shards, -0.22, 0.18) if shards else 1.0
    array = jax.random.normal(stream_key, dims, jnp.float32) * deviation * level
    return jnp.minimum(jnp.maximum(array, -most), most).astype(kind)


def setup_inputs(seed: int = 0, part: int = 0) -> dict:
    key_list = jax.random.split(jax.random.key(seed), 12)
    part_splits = jax.random.split(jax.random.fold_in(key_list[11], part), 12)
    span_q = draw_span_q(jax.random.fold_in(jax.random.fold_in(key_list[11], part), 71), part)
    span_kv = bell_draw(part_splits[1], (SPANS, 2, SPAN, KVH * HD), 1.0, 6.0, ((0, 4), (3, 4)))
    span_offset = draw_span_offset(jax.random.fold_in(jax.random.fold_in(key_list[11], part), 71), part)
    span_length = draw_span_length(jax.random.fold_in(jax.random.fold_in(key_list[11], part), 71), part)
    span_dest = draw_span_dest(jax.random.fold_in(jax.random.fold_in(key_list[11], part), 71), part)
    prefix_kv = bell_draw(part_splits[5], (NBLK, 2, BLK, KVH * HD), 1.0, 6.0, ((0, 4), (3, 4)))
    resident_kv = bell_draw(part_splits[6], (SEQS, 2, RES, KVH * HD), 1.0, 6.0, ((0, 4), (3, 4)))
    seq_length = draw_seq_length(jax.random.fold_in(jax.random.fold_in(key_list[11], part), 71), part)
    decode_q = draw_decode_q(jax.random.fold_in(jax.random.fold_in(key_list[11], part), 71), part)
    decode_kv = bell_draw(part_splits[9], (SEQS, 2, STEPS, KVH * HD), 1.0, 6.0, ((0, 4), (3, 4)))
    block_target = draw_block_target(jax.random.fold_in(jax.random.fold_in(key_list[11], part), 71), part)
    return {"span_q": span_q, "span_kv": span_kv, "span_offset": span_offset, "span_length": span_length, "span_dest": span_dest, "prefix_kv": prefix_kv, "resident_kv": resident_kv, "seq_length": seq_length, "decode_q": decode_q, "decode_kv": decode_kv, "block_target": block_target}


masked_low = -1e+30

def softmax_parts(scores, allowed):
    masked = jnp.where(allowed, scores, masked_low)
    highest = lax.optimization_barrier(jnp.max(masked, axis=-1, keepdims=True))
    expons = jnp.where(allowed, jnp.exp(masked - highest), 0.0)
    return (expons, lax.optimization_barrier(jnp.sum(expons, axis=-1)))

def reference(span_q, span_kv, span_offset, span_length, span_dest, prefix_kv, resident_kv, seq_length, decode_q, decode_kv, block_target):
    scaling = 1.0 / math.sqrt(HD)
    cached = prefix_kv.reshape(N_POOL, PB, 2, BLK, KVH, HD).transpose(0, 2, 1, 3, 4, 5).reshape(N_POOL, 2, PREF, KVH, HD)

    def one_span(pieces):
        queries, span_pair, offset, length, target = pieces
        owned = lax.dynamic_index_in_dim(cached, target, 0, keepdims=False)
        own_pair = span_pair.reshape(2, SPAN, KVH, HD)
        keys = jnp.concatenate([owned[0], own_pair[0]], axis=0).astype(jnp.float32)
        values = jnp.concatenate([owned[1], own_pair[1]], axis=0).astype(jnp.float32)
        query_f = queries.reshape(SPAN, KVH, QPK, HD).astype(jnp.float32)
        scores = jnp.einsum('ikgd,jkd->kgij', query_f, keys) * scaling
        position = jnp.arange(PREF + SPAN)
        row_index = jnp.arange(SPAN)
        in_span = position - PREF
        allowed = jnp.where(position[None, :] < PREF, position[None, :] < offset, (in_span[None, :] <= row_index[:, None]) & (in_span[None, :] < length))
        expons, totals = softmax_parts(scores, allowed)
        weights = lax.optimization_barrier(expons.astype(jnp.bfloat16)).astype(jnp.float32)
        blended = jnp.einsum('kgij,jkd->ikgd', weights, values) / jnp.transpose(totals, (2, 0, 1))[..., None]
        blended = jnp.where((row_index < length)[:, None, None, None], blended, 0.0)
        return blended.astype(jnp.bfloat16).reshape(SPAN, QH * HD)
    prefill_out = lax.map(one_span, (span_q, span_kv, span_offset, span_length, span_dest))
    moved_keys = prefix_kv[:, 0].reshape(NBLK * BLK, KVH, HD).astype(jnp.float32)
    moved_values = prefix_kv[:, 1].reshape(NBLK * BLK, KVH, HD).astype(jnp.float32)
    key_owner = jnp.repeat(block_target, BLK)

    def one_sequence(pieces):
        queries, resident_pair, step_pair, length, seq_id = pieces
        query_f = queries.reshape(STEPS, KVH, QPK, HD).astype(jnp.float32)
        res_pair = resident_pair.reshape(2, RES, KVH, HD).astype(jnp.float32)
        new_pair = step_pair.reshape(2, STEPS, KVH, HD).astype(jnp.float32)
        score_res = jnp.einsum('tkgd,jkd->ktgj', query_f, res_pair[0]) * scaling
        score_mov = jnp.einsum('tkgd,jkd->ktgj', query_f, moved_keys) * scaling
        score_new = jnp.einsum('tkgd,jkd->ktgj', query_f, new_pair[0]) * scaling
        scores = jnp.concatenate([score_res, score_mov, score_new], axis=-1)
        step_index = jnp.arange(STEPS)
        allow_res = jnp.broadcast_to((jnp.arange(RES) < length)[None, :], (STEPS, RES))
        allow_mov = jnp.broadcast_to((key_owner == seq_id)[None, :], (STEPS, NBLK * BLK))
        allow_new = step_index[None, :] <= step_index[:, None]
        allowed = jnp.concatenate([allow_res, allow_mov, allow_new], axis=-1)[None, :, None, :]
        expons, totals = softmax_parts(scores, allowed)
        blended = jnp.einsum('ktgj,jkd->tkgd', expons[..., :RES], res_pair[1], precision=lax.Precision.HIGHEST)
        blended = blended + jnp.einsum('ktgj,jkd->tkgd', expons[..., RES:RES + NBLK * BLK], moved_values, precision=lax.Precision.HIGHEST)
        blended = blended + jnp.einsum('ktgj,jkd->tkgd', expons[..., RES + NBLK * BLK:], new_pair[1], precision=lax.Precision.HIGHEST)
        blended = blended / jnp.transpose(totals, (1, 0, 2))[..., None]
        return blended.astype(jnp.bfloat16).reshape(STEPS, QH * HD)
    seq_ids = jnp.arange(SEQS, dtype=jnp.int32)
    decode_out = lax.map(one_sequence, (decode_q, resident_kv, decode_kv, seq_length, seq_ids))
    return (prefill_out, decode_out)
```

```python
import functools

import jax
import jax.numpy as jnp
from jax import lax
from jax.experimental import pallas as pl
from jax.experimental.pallas import tpu as pltpu
from jax.sharding import PartitionSpec as P

HD = 128
SCALE = HD ** (-0.5)
LOW = -1e30
GAP = 16
NT = (((1,), (1,)), ((), ()))
NN = (((1,), (0,)), ((), ()))


def split_bf16(x):
    high = x.astype(jnp.bfloat16).astype(jnp.float32)
    rest = x - high
    mid = rest.astype(jnp.bfloat16).astype(jnp.float32)
    return high, mid, rest - mid


def pack_stats(top, total):
    a, b, c = split_bf16(top)
    d, e, _ = split_bf16(total)
    out = a + pltpu.roll(b, GAP, 1) + pltpu.roll(c, 2 * GAP, 1)
    out = out + pltpu.roll(d, 3 * GAP, 1) + pltpu.roll(e, 4 * GAP, 1)
    return out.astype(jnp.bfloat16)


def unpack_stats(packed):
    t = packed.astype(jnp.float32)
    top = t + pltpu.roll(t, 128 - GAP, 1) + pltpu.roll(t, 128 - 2 * GAP, 1)
    total = pltpu.roll(t, 128 - 3 * GAP, 1) + pltpu.roll(t, 128 - 4 * GAP, 1)
    return top, total


def soft(scores):
    top = jnp.max(scores, axis=-1, keepdims=True)
    weights = jnp.exp((scores - top) * SCALE)
    return top, weights.astype(jnp.bfloat16), jnp.sum(weights, axis=-1, keepdims=True)


def kernel(
    n, cap, rows, heads, sharing, steps,
    from_ref, back_ref, offset_ref, length_ref, seqlen_ref,
    target_ref, span_q, span_kv, prefix, resident, decode_q, decode_kv,
    prefill_out, decode_out,
    keys, values, res, own_kv, q_send, q_recv, m_send, m_recv, r_send, r_recv,
    self_acc, self_top, self_total,
    q_ssem, q_rsem, m_ssem, m_rsem, r_ssem, r_rsem, loc_sem,
):
    me = lax.axis_index("pool")
    spans = span_q.shape[0]
    seqs = resident.shape[0]
    per = cap + 1
    width = heads * sharing * HD
    tall = sharing * rows

    def at(step):
        return lax.rem(me + step, n)

    loads = []
    for k in range(heads):
        cols = pl.ds(k * HD, HD)
        loads.append(pltpu.make_async_copy(prefix.at[:, 0, :, cols], keys.at[k], loc_sem.at[2 * k]))
        loads.append(pltpu.make_async_copy(prefix.at[:, 1, :, cols], values.at[k], loc_sem.at[2 * k + 1]))
    own_load = pltpu.make_async_copy(span_kv, own_kv, loc_sem.at[2 * heads])
    res_load = pltpu.make_async_copy(resident, res, loc_sem.at[2 * heads + 1])
    for load in loads:
        load.start()
    own_load.start()
    res_load.start()

    barrier = pltpu.get_barrier_semaphore()

    @pl.loop(1, n)
    def _(d):
        pl.semaphore_signal(barrier, inc=1, device_id={"pool": at(d)}, device_id_type=pl.DeviceIdType.MESH)

    def fill(buf, meta, d):
        @pl.loop(0, cap)
        def _(r):
            pick = from_ref[d * cap + r]
            buf[d * per + r] = span_q[pick]
            meta[d, pl.ds(r, 1), :] = jnp.full((1, 128), offset_ref[pick], jnp.int32)

        buf[d * per + cap] = decode_q[...]

    def q_copy(d, to):
        return pltpu.make_async_remote_copy(
            src_ref=q_send.at[pl.ds(d * per, per)],
            dst_ref=q_recv.at[pl.ds(d * per, per)],
            send_sem=q_ssem.at[d], recv_sem=q_rsem.at[d],
            device_id={"pool": to}, device_id_type=pl.DeviceIdType.MESH,
        )

    def m_copy(d, to):
        return pltpu.make_async_remote_copy(
            src_ref=m_send.at[d], dst_ref=m_recv.at[d],
            send_sem=m_ssem.at[d], recv_sem=m_rsem.at[d],
            device_id={"pool": to}, device_id_type=pl.DeviceIdType.MESH,
        )

    def r_copy(d, to):
        return pltpu.make_async_remote_copy(
            src_ref=r_send.at[pl.ds(d * per, per)],
            dst_ref=r_recv.at[pl.ds(d * per, per)],
            send_sem=r_ssem.at[d], recv_sem=r_rsem.at[d],
            device_id={"pool": to}, device_id_type=pl.DeviceIdType.MESH,
        )

    m_send[...] = jnp.zeros_like(m_send)
    m_recv[0] = jnp.zeros(m_recv.shape[1:], jnp.int32)
    pl.semaphore_wait(barrier, n - 1)

    @pl.loop(1, n)
    def _(d):
        fill(q_send, m_send, d)
        m_copy(d, at(d)).start()
        q_copy(d, at(d)).start()

    fill(q_recv, m_recv, 0)

    lane = lax.broadcasted_iota(jnp.int32, (rows, 128), 1)

    def stacked(block, k):
        base = k * sharing * HD
        return jnp.concatenate(
            [block[:, base + g * HD : base + (g + 1) * HD] for g in range(sharing)], axis=0
        )

    def spread(tops, totals, top, total, k):
        for g in range(sharing):
            h = k * sharing + g
            part = slice(g * rows, (g + 1) * rows)
            tops = jnp.where(lane == h, top[part], tops)
            totals = jnp.where(lane == h, total[part], totals)
        return tops, totals

    def attend(buf, out, slot, bias):
        block = buf[slot]
        tops = totals = jnp.zeros((rows, 128), jnp.float32)
        for k in range(heads):
            query = stacked(block, k)
            key = keys[k].reshape(-1, HD)
            value = values[k].reshape(-1, HD)
            score = lax.dot_general(query, key, NT, preferred_element_type=jnp.float32)
            if bias.shape[0] == 1:
                score = score + bias
            else:
                score = (score.reshape(sharing, rows, -1) + bias[None]).reshape(tall, -1)
            top, weight, total = soft(score)
            acc = lax.dot_general(weight, value, NN, preferred_element_type=jnp.float32)
            for g in range(sharing):
                h = k * sharing + g
                out[slot, :, h * HD : (h + 1) * HD] = acc[g * rows : (g + 1) * rows].astype(jnp.bfloat16)
            tops, totals = spread(tops, totals, top, total, k)
        out[slot, :, width:] = pack_stats(tops, totals)

    tokens = keys.shape[1] * keys.shape[2]
    position = lax.broadcasted_iota(jnp.int32, (1, tokens), 1)

    def chunk(out, d):
        @pl.loop(0, cap)
        def _(r):
            limit = m_recv[d, pl.ds(r, 1), :][:, :1]
            attend(q_recv, out, d * per + r, jnp.where(position < limit, 0.0, LOW))

        source = lax.rem(me - d + n, n)
        seq = source * seqs + lax.broadcasted_iota(jnp.int32, (rows, 1), 0) // steps
        attend(q_recv, out, d * per + cap, jnp.where(target_ref[...] == seq, 0.0, LOW))

    for load in loads:
        load.wait()
    chunk(r_recv, 0)

    own_load.wait()
    row_of = lax.rem(lax.broadcasted_iota(jnp.int32, (tall, rows), 0), rows)
    col_of = lax.broadcasted_iota(jnp.int32, (tall, rows), 1)

    def keep(index, k, acc, tops, totals, top, total):
        for g in range(sharing):
            h = k * sharing + g
            self_acc[index, :, h * HD : (h + 1) * HD] = acc[g * rows : (g + 1) * rows]
        return spread(tops, totals, top, total, k)

    @pl.loop(0, spans)
    def _(j):
        block = span_q[j]
        tops = totals = jnp.zeros((rows, 128), jnp.float32)
        for k in range(heads):
            cols = slice(k * HD, (k + 1) * HD)
            score = lax.dot_general(
                stacked(block, k), own_kv[j, 0, :, cols], NT, preferred_element_type=jnp.float32
            )
            top, weight, total = soft(jnp.where(col_of <= row_of, score, LOW))
            acc = lax.dot_general(weight, own_kv[j, 1, :, cols], NN, preferred_element_type=jnp.float32)
            tops, totals = keep(j, k, acc, tops, totals, top, total)
        self_top[j] = tops
        self_total[j] = totals

    res_load.wait()
    res_len = resident.shape[2]
    slot_of = lax.broadcasted_iota(jnp.int32, (1, res_len), 1)
    row_seq = lax.rem(lax.broadcasted_iota(jnp.int32, (tall, 1), 0), rows) // steps
    tops = totals = jnp.zeros((rows, 128), jnp.float32)
    for k in range(heads):
        cols = slice(k * HD, (k + 1) * HD)
        query = stacked(decode_q[...], k)

        def one(s, carry):
            acc, top, total = carry
            score = lax.dot_general(query, res[s, 0, :, cols], NT, preferred_element_type=jnp.float32)
            score = score + jnp.where(slot_of < seqlen_ref[s], 0.0, LOW)
            top_s, weight, total_s = soft(score)
            acc_s = lax.dot_general(weight, res[s, 1, :, cols], NN, preferred_element_type=jnp.float32)
            here = row_seq == s
            return jnp.where(here, acc_s, acc), jnp.where(here, top_s, top), jnp.where(here, total_s, total)

        zero = jnp.zeros((tall, 1), jnp.float32)
        acc, top, total = lax.fori_loop(0, seqs, one, (jnp.zeros((tall, HD), jnp.float32), zero, zero))
        score = lax.dot_general(query, decode_kv[0, :, cols], NT, preferred_element_type=jnp.float32)
        fits = (col_of // steps == row_of // steps) & (col_of <= row_of)
        top_n, weight, total_n = soft(jnp.where(fits, score, LOW))
        acc_n = lax.dot_general(weight, decode_kv[1, :, cols], NN, preferred_element_type=jnp.float32)
        best = jnp.maximum(top, top_n)
        a = jnp.exp((top - best) * SCALE)
        b = jnp.exp((top_n - best) * SCALE)
        tops, totals = keep(spans, k, acc * a + acc_n * b, tops, totals, best, total * a + total_n * b)
    self_top[spans] = tops
    self_total[spans] = totals

    @pl.loop(1, n)
    def _(d):
        source = lax.rem(me - d + n, n)
        m_copy(d, at(d)).wait_recv()
        q_copy(d, at(d)).wait_recv()
        chunk(r_send, d)
        r_copy(d, source).start()

    @pl.loop(1, n)
    def _(d):
        source = lax.rem(me - d + n, n)
        m_copy(d, at(d)).wait_send()
        q_copy(d, at(d)).wait_send()
        r_copy(d, source).wait_recv()

    live_row = lax.broadcasted_iota(jnp.int32, (rows, 128), 0)

    @pl.loop(0, spans)
    def _(j):
        back = back_ref[j]
        got = r_recv[back]
        top, total = unpack_stats(got[:, width:])
        own = self_top[j]
        best = jnp.maximum(top, own)
        a = jnp.exp((top - best) * SCALE)
        b = jnp.exp((own - best) * SCALE)
        share = total * a + self_total[j] * b
        live = live_row < length_ref[j]
        share = jnp.where(lane < heads * sharing, share, 1.0)
        a = jnp.where(live, a / share, 0.0)
        b = jnp.where(live, b / share, 0.0)
        for h in range(heads * sharing):
            cols = slice(h * HD, (h + 1) * HD)
            out = got[:, cols].astype(jnp.float32) * a[:, h : h + 1] + self_acc[j, :, cols] * b[:, h : h + 1]
            prefill_out[j, :, cols] = out.astype(jnp.bfloat16)

    @pl.loop(0, n)
    def _(d):
        got = r_recv[d * per + cap]
        top, total = unpack_stats(got[:, width:])
        own = self_top[spans]
        best = jnp.maximum(top, own)
        a = jnp.exp((top - best) * SCALE)
        b = jnp.exp((own - best) * SCALE)
        for h in range(heads * sharing):
            cols = slice(h * HD, (h + 1) * HD)
            self_acc[spans, :, cols] = (
                got[:, cols].astype(jnp.float32) * a[:, h : h + 1]
                + self_acc[spans, :, cols] * b[:, h : h + 1]
            )
        self_total[spans] = total * a + self_total[spans] * b
        self_top[spans] = best

    share = self_total[spans]
    for h in range(heads * sharing):
        cols = slice(h * HD, (h + 1) * HD)
        decode_out[:, cols] = (self_acc[spans, :, cols] / share[:, h : h + 1]).astype(jnp.bfloat16)

    @pl.loop(1, n)
    def _(d):
        r_copy(d, lax.rem(me - d + n, n)).wait_send()


def on_device(
    span_q, span_kv, span_offset, span_length, span_dest, prefix_kv,
    resident_kv, seq_length, decode_q, decode_kv, block_target,
):
    n = lax.axis_size("pool")
    me = lax.axis_index("pool")
    spans, rows, width = span_q.shape
    kv_width = span_kv.shape[-1]
    heads = kv_width // HD
    sharing = width // kv_width
    seqs, steps = decode_q.shape[:2]
    blocks, _, block_len, _ = prefix_kv.shape
    cap = -(-spans // n)
    per = cap + 1
    cap_pad = -(-cap // 8) * 8

    shift = lax.rem(span_dest - me + n, n)
    order = jnp.arange(spans, dtype=jnp.int32)
    before = (shift[None, :] == shift[:, None]) & (order[None, :] < order[:, None])
    rank = jnp.sum(before.astype(jnp.int32), axis=1)
    placed = shift * cap + rank
    back = shift * per + rank
    slots = jnp.arange(n * cap, dtype=jnp.int32)
    source = jnp.sum(jnp.where(placed[None, :] == slots[:, None], order[None, :], 0), axis=1)
    targets = jnp.repeat(block_target, block_len)[None, :]
    decode_pair = jnp.transpose(decode_kv, (1, 0, 2, 3)).reshape(2, seqs * steps, kv_width)
    decode_rows = decode_q.reshape(seqs * steps, width)

    bf = jnp.bfloat16
    smem = pl.BlockSpec(memory_space=pltpu.SMEM)
    vmem = pl.BlockSpec(memory_space=pltpu.VMEM)
    hbm = pl.BlockSpec(memory_space=pl.ANY)
    prefill_out, decode_out = pl.pallas_call(
        functools.partial(kernel, n, cap, rows, heads, sharing, steps),
        out_shape=(
            jax.ShapeDtypeStruct((spans, rows, width), bf),
            jax.ShapeDtypeStruct((seqs * steps, width), bf),
        ),
        in_specs=[smem] * 5 + [vmem, vmem, hbm, hbm, hbm, vmem, vmem],
        out_specs=(vmem, vmem),
        scratch_shapes=[
            pltpu.VMEM((heads, blocks, block_len, HD), bf),
            pltpu.VMEM((heads, blocks, block_len, HD), bf),
            pltpu.VMEM(resident_kv.shape, bf),
            pltpu.VMEM(span_kv.shape, bf),
            pltpu.VMEM((n * per, rows, width), bf),
            pltpu.VMEM((n * per, rows, width), bf),
            pltpu.VMEM((n, cap_pad, 128), jnp.int32),
            pltpu.VMEM((n, cap_pad, 128), jnp.int32),
            pltpu.VMEM((n * per, rows, width + 128), bf),
            pltpu.VMEM((n * per, rows, width + 128), bf),
            pltpu.VMEM((spans + 1, rows, width), jnp.float32),
            pltpu.VMEM((spans + 1, rows, 128), jnp.float32),
            pltpu.VMEM((spans + 1, rows, 128), jnp.float32),
        ]
        + [pltpu.SemaphoreType.DMA((n,))] * 6
        + [pltpu.SemaphoreType.DMA((2 * heads + 2,))],
        compiler_params=pltpu.CompilerParams(
            collective_id=0, has_side_effects=True, vmem_limit_bytes=56 * 2**20
        ),
        cost_estimate=pl.CostEstimate(
            flops=4 * (spans + cap) * rows * width * blocks * block_len,
            bytes_accessed=12 * 2**20,
            transcendentals=(spans + cap) * rows * heads * sharing * blocks * block_len,
        ),
    )(
        source, back, span_offset, span_length, seq_length,
        targets, span_q, span_kv, prefix_kv, resident_kv, decode_rows, decode_pair,
    )
    return prefill_out, decode_out.reshape(seqs, steps, width)


def solution(mesh):
    return jax.shard_map(
        on_device,
        mesh=mesh,
        in_specs=(
            P(("groups", "pool"), None, "tp"),
            P(("groups", "pool"), None, None, "tp"),
            P(("groups", "pool")),
            P(("groups", "pool")),
            P(("groups", "pool")),
            P(("groups", "pool"), None, None, "tp"),
            P(("groups", "pool"), None, None, "tp"),
            P(("groups", "pool")),
            P(("groups", "pool"), None, "tp"),
            P(("groups", "pool"), None, None, "tp"),
            P(("groups", "pool")),
        ),
        out_specs=(P(("groups", "pool"), None, "tp"), P(("groups", "pool"), None, "tp")),
        check_vma=False,
    )
```

```python
import functools

import jax
import jax.numpy as jnp
from jax import lax
from jax.experimental import pallas as pl
from jax.experimental.pallas import tpu as pltpu
from jax.sharding import PartitionSpec as P

HD = 128
SCALE = HD ** (-0.5)
LOW = -1e30
NT = (((1,), (1,)), ((), ()))
NN = (((1,), (0,)), ((), ()))


def soft(scores):
    top = jnp.max(scores, axis=-1, keepdims=True)
    weights = jnp.exp((scores - top) * SCALE)
    return top, weights.astype(jnp.bfloat16), jnp.sum(weights, axis=-1, keepdims=True)


def kernel(
    n, cap, rows, heads, sharing, steps,
    dest_ref, offset_ref, length_ref, seqlen_ref, target_ref,
    span_q, span_kv, prefix, resident, step_q, step_kv,
    prefill_out, decode_out,
    keys, values, res, own_kv, q_send, q_recv, m_send, m_recv, r_send, r_recv,
    t_send, t_recv, self_acc, self_top, self_total, target_row, decode_q, decode_pair, new_kv,
    q_ssem, q_rsem, m_ssem, m_rsem, r_ssem, r_rsem, t_ssem, t_rsem, loc_sem,
):
    me = lax.axis_index("pool")
    spans = span_q.shape[0]
    seqs = resident.shape[0]
    per = cap + 1
    width = heads * sharing * HD
    tall = sharing * rows
    count = heads * sharing
    block_len = prefix.shape[2]

    def at(step):
        return lax.rem(me + step, n)

    loads = []
    for k in range(heads):
        cols = pl.ds(k * HD, HD)
        loads.append(pltpu.make_async_copy(prefix.at[:, 0, :, cols], keys.at[k], loc_sem.at[2 * k]))
        loads.append(pltpu.make_async_copy(prefix.at[:, 1, :, cols], values.at[k], loc_sem.at[2 * k + 1]))
    own_load = pltpu.make_async_copy(span_kv, own_kv, loc_sem.at[2 * heads])
    res_load = pltpu.make_async_copy(resident, res, loc_sem.at[2 * heads + 1])
    for load in loads:
        load.start()
    own_load.start()
    res_load.start()

    barrier = pltpu.get_barrier_semaphore()

    @pl.loop(1, n)
    def _(d):
        pl.semaphore_signal(barrier, inc=1, device_id={"pool": at(d)}, device_id_type=pl.DeviceIdType.MESH)

    def shift_of(j):
        away = dest_ref[j] - me
        return jnp.where(away < 0, away + n, away)

    def span_at(d, r):
        pick = seen = jnp.int32(0)
        for j in range(spans):
            hit = shift_of(j) == d
            pick = jnp.where(hit & (seen == r), j, pick)
            seen = seen + hit.astype(jnp.int32)
        return pick

    def rank_of(j):
        rank = jnp.int32(0)
        for i in range(spans):
            rank = rank + ((dest_ref[i] == dest_ref[j]) & (i < j)).astype(jnp.int32)
        return jnp.minimum(rank, cap - 1)

    def fill(buf, meta, d):
        @pl.loop(0, cap)
        def _(r):
            pick = span_at(d, r)
            buf[d * per + r] = span_q[pick]
            meta[d, pl.ds(r, 1), :] = jnp.full((1, 128), offset_ref[pick], jnp.int32)

        buf[d * per + cap] = decode_q[...]

    def q_copy(d, to):
        return pltpu.make_async_remote_copy(
            src_ref=q_send.at[pl.ds(d * per, per)],
            dst_ref=q_recv.at[pl.ds(d * per, per)],
            send_sem=q_ssem.at[d], recv_sem=q_rsem.at[d],
            device_id={"pool": to}, device_id_type=pl.DeviceIdType.MESH,
        )

    def m_copy(d, to):
        return pltpu.make_async_remote_copy(
            src_ref=m_send.at[d], dst_ref=m_recv.at[d],
            send_sem=m_ssem.at[d], recv_sem=m_rsem.at[d],
            device_id={"pool": to}, device_id_type=pl.DeviceIdType.MESH,
        )

    def t_copy(d, to):
        return pltpu.make_async_remote_copy(
            src_ref=t_send.at[d], dst_ref=t_recv.at[d],
            send_sem=t_ssem.at[d], recv_sem=t_rsem.at[d],
            device_id={"pool": to}, device_id_type=pl.DeviceIdType.MESH,
        )

    def near(i):
        odd = lax.rem(i, 2)
        return odd * ((i + 1) // 2) + (1 - odd) * (n - i // 2)

    def r_copy(d, to):
        return pltpu.make_async_remote_copy(
            src_ref=r_send.at[pl.ds(d * per, per)],
            dst_ref=r_recv.at[pl.ds(d * per, per)],
            send_sem=r_ssem.at[d], recv_sem=r_rsem.at[d],
            device_id={"pool": to}, device_id_type=pl.DeviceIdType.MESH,
        )

    for s in range(seqs):
        part = slice(s * steps, (s + 1) * steps)
        decode_pair[part, :] = step_q[s].astype(jnp.float32)
        for k in range(2):
            new_kv[k, part, :] = step_kv[s, k].astype(jnp.float32)
    decode_q[...] = decode_pair[...].astype(jnp.bfloat16)
    m_send[...] = jnp.zeros_like(m_send)
    m_recv[0] = jnp.zeros(m_recv.shape[1:], jnp.int32)
    pl.semaphore_wait(barrier, n - 1)

    @pl.loop(1, n)
    def _(i):
        d = near(i)
        fill(q_send, m_send, d)
        m_copy(d, at(d)).start()
        q_copy(d, at(d)).start()

    fill(q_recv, m_recv, 0)
    for b in range(prefix.shape[0]):
        target_row[:, b * block_len : (b + 1) * block_len] = jnp.full((8, block_len), target_ref[b], jnp.int32)

    lane = lax.broadcasted_iota(jnp.int32, (rows, 128), 1)

    def stacked(block, k):
        base = k * sharing * HD
        return jnp.concatenate(
            [block[:, base + g * HD : base + (g + 1) * HD] for g in range(sharing)], axis=0
        )

    def spread(tops, totals, top, total, k):
        for g in range(sharing):
            h = k * sharing + g
            part = slice(g * rows, (g + 1) * rows)
            tops = jnp.where(lane == h, top[part], tops)
            totals = jnp.where(lane == h, total[part], totals)
        return tops, totals

    def attend(buf, out, stats, d, r, bias):
        slot = d * per + r
        block = buf[slot]
        tile = stats[d]
        for k in range(heads):
            query = stacked(block, k)
            key = keys[k].reshape(-1, HD)
            value = values[k].reshape(-1, HD)
            score = lax.dot_general(query, key, NT, preferred_element_type=jnp.float32)
            if bias.shape[0] == 1:
                score = score + bias
            else:
                score = (score.reshape(sharing, rows, -1) + bias[None]).reshape(tall, -1)
            top, weight, total = soft(score)
            acc = lax.dot_general(weight, value, NN, preferred_element_type=jnp.float32)
            for g in range(sharing):
                h = k * sharing + g
                out[slot, :, h * HD : (h + 1) * HD] = acc[g * rows : (g + 1) * rows].astype(jnp.bfloat16)
            for g in range(sharing):
                part = slice(g * rows, (g + 1) * rows)
                spot = r * 2 * count + k * sharing + g
                tile = jnp.where(lane == spot, top[part], tile)
                tile = jnp.where(lane == spot + count, total[part], tile)
        stats[d] = tile

    tokens = keys.shape[1] * keys.shape[2]
    position = lax.broadcasted_iota(jnp.int32, (1, tokens), 1)

    def chunk(out, stats, d):
        stats[d] = jnp.zeros((rows, 128), jnp.float32)

        @pl.loop(0, cap)
        def _(r):
            limit = m_recv[d, pl.ds(r, 1), :][:, :1]
            attend(q_recv, out, stats, d, r, jnp.where(position < limit, 0.0, LOW))

        source = lax.rem(me - d + n, n)
        seq = source * seqs + lax.broadcasted_iota(jnp.int32, (rows, 1), 0) // steps
        attend(q_recv, out, stats, d, cap, jnp.where(target_row[0:1, :] == seq, 0.0, LOW))

    for load in loads:
        load.wait()
    chunk(r_recv, t_recv, 0)

    @pl.loop(1, n)
    def _(i):
        d = near(i)
        source = lax.rem(me - d + n, n)
        m_copy(d, at(d)).wait_recv()
        q_copy(d, at(d)).wait_recv()
        chunk(r_send, t_send, d)
        t_copy(d, source).start()
        r_copy(d, source).start()

    own_load.wait()
    row_of = lax.rem(lax.broadcasted_iota(jnp.int32, (tall, rows), 0), rows)
    col_of = lax.broadcasted_iota(jnp.int32, (tall, rows), 1)

    def keep(index, k, acc, tops, totals, top, total):
        for g in range(sharing):
            h = k * sharing + g
            self_acc[index, :, h * HD : (h + 1) * HD] = acc[g * rows : (g + 1) * rows]
        return spread(tops, totals, top, total, k)

    @pl.loop(0, spans)
    def _(j):
        block = span_q[j]
        tops = totals = jnp.zeros((rows, 128), jnp.float32)
        for k in range(heads):
            cols = slice(k * HD, (k + 1) * HD)
            score = lax.dot_general(
                stacked(block, k), own_kv[j, 0, :, cols], NT, preferred_element_type=jnp.float32
            )
            top, weight, total = soft(jnp.where(col_of <= row_of, score, LOW))
            acc = lax.dot_general(weight, own_kv[j, 1, :, cols], NN, preferred_element_type=jnp.float32)
            tops, totals = keep(j, k, acc, tops, totals, top, total)
        self_top[j] = tops
        self_total[j] = totals

    res_load.wait()
    res_len = resident.shape[2]
    slot_of = lax.broadcasted_iota(jnp.int32, (1, res_len), 1)
    row_seq = lax.rem(lax.broadcasted_iota(jnp.int32, (tall, 1), 0), rows) // steps
    tops = totals = jnp.zeros((rows, 128), jnp.float32)
    for k in range(heads):
        cols = slice(k * HD, (k + 1) * HD)
        query = stacked(decode_q[...], k)

        def one(s, carry):
            acc, top, total = carry
            score = lax.dot_general(query, res[s, 0, :, cols], NT, preferred_element_type=jnp.float32)
            score = score + jnp.where(slot_of < seqlen_ref[s], 0.0, LOW)
            top_s, weight, total_s = soft(score)
            acc_s = lax.dot_general(weight, res[s, 1, :, cols], NN, preferred_element_type=jnp.float32)
            here = row_seq == s
            return jnp.where(here, acc_s, acc), jnp.where(here, top_s, top), jnp.where(here, total_s, total)

        zero = jnp.zeros((tall, 1), jnp.float32)
        acc, top, total = lax.fori_loop(0, seqs, one, (jnp.zeros((tall, HD), jnp.float32), zero, zero))
        score = lax.dot_general(query, new_kv[0, :, cols].astype(jnp.bfloat16), NT, preferred_element_type=jnp.float32)
        fits = (col_of // steps == row_of // steps) & (col_of <= row_of)
        top_n, weight, total_n = soft(jnp.where(fits, score, LOW))
        acc_n = lax.dot_general(weight, new_kv[1, :, cols].astype(jnp.bfloat16), NN, preferred_element_type=jnp.float32)
        best = jnp.maximum(top, top_n)
        a = jnp.exp((top - best) * SCALE)
        b = jnp.exp((top_n - best) * SCALE)
        tops, totals = keep(spans, k, acc * a + acc_n * b, tops, totals, best, total * a + total_n * b)
    self_top[spans] = tops
    self_total[spans] = totals

    @pl.loop(1, n)
    def _(d):
        source = lax.rem(me - d + n, n)
        m_copy(d, at(d)).wait_send()
        q_copy(d, at(d)).wait_send()
        t_copy(d, source).wait_recv()
        r_copy(d, source).wait_recv()

    def stats_of(tile, rank):
        top = tile
        for r in range(1, per):
            top = jnp.where(rank == r, pltpu.roll(tile, 128 - r * 2 * count, 1), top)
        return top, pltpu.roll(top, 128 - count, 1)

    live_row = lax.broadcasted_iota(jnp.int32, (rows, 128), 0)

    @pl.loop(0, spans)
    def _(j):
        away = shift_of(j)
        rank = rank_of(j)
        got = r_recv[away * per + rank]
        top, total = stats_of(t_recv[away], rank)
        own = self_top[j]
        best = jnp.maximum(top, own)
        a = jnp.exp((top - best) * SCALE)
        b = jnp.exp((own - best) * SCALE)
        share = total * a + self_total[j] * b
        live = live_row < length_ref[j]
        share = jnp.where(lane < count, share, 1.0)
        a = jnp.where(live, a / share, 0.0)
        b = jnp.where(live, b / share, 0.0)
        for h in range(heads * sharing):
            cols = slice(h * HD, (h + 1) * HD)
            out = got[:, cols].astype(jnp.float32) * a[:, h : h + 1] + self_acc[j, :, cols] * b[:, h : h + 1]
            prefill_out[j, :, cols] = out.astype(jnp.bfloat16)

    @pl.loop(0, n)
    def _(d):
        got = r_recv[d * per + cap]
        top, total = stats_of(t_recv[d], cap)
        own = self_top[spans]
        best = jnp.maximum(top, own)
        a = jnp.exp((top - best) * SCALE)
        b = jnp.exp((own - best) * SCALE)
        for h in range(heads * sharing):
            cols = slice(h * HD, (h + 1) * HD)
            self_acc[spans, :, cols] = (
                got[:, cols].astype(jnp.float32) * a[:, h : h + 1]
                + self_acc[spans, :, cols] * b[:, h : h + 1]
            )
        self_total[spans] = total * a + self_total[spans] * b
        self_top[spans] = best

    share = self_total[spans]
    for h in range(count):
        cols = slice(h * HD, (h + 1) * HD)
        decode_pair[:, cols] = self_acc[spans, :, cols] / share[:, h : h + 1]
    for s in range(seqs):
        decode_out[s] = decode_pair[s * steps : (s + 1) * steps, :].astype(jnp.bfloat16)

    @pl.loop(1, n)
    def _(d):
        t_copy(d, lax.rem(me - d + n, n)).wait_send()
        r_copy(d, lax.rem(me - d + n, n)).wait_send()


def on_device(
    span_q, span_kv, span_offset, span_length, span_dest, prefix_kv,
    resident_kv, seq_length, decode_q, decode_kv, block_target,
):
    n = lax.axis_size("pool")
    spans, rows, width = span_q.shape
    kv_width = span_kv.shape[-1]
    heads = kv_width // HD
    sharing = width // kv_width
    seqs, steps = decode_q.shape[:2]
    blocks, _, block_len, _ = prefix_kv.shape
    cap = -(-spans // n)
    per = cap + 1
    cap_pad = -(-cap // 8) * 8

    bf = jnp.bfloat16
    smem = pl.BlockSpec(memory_space=pltpu.SMEM)
    vmem = pl.BlockSpec(memory_space=pltpu.VMEM)
    hbm = pl.BlockSpec(memory_space=pl.ANY)
    prefill_out, decode_out = pl.pallas_call(
        functools.partial(kernel, n, cap, rows, heads, sharing, steps),
        out_shape=(
            jax.ShapeDtypeStruct((spans, rows, width), bf),
            jax.ShapeDtypeStruct((seqs, steps, width), bf),
        ),
        in_specs=[smem] * 5 + [vmem, hbm, hbm, hbm, vmem, vmem],
        out_specs=(vmem, vmem),
        scratch_shapes=[
            pltpu.VMEM((heads, blocks, block_len, HD), bf),
            pltpu.VMEM((heads, blocks, block_len, HD), bf),
            pltpu.VMEM(resident_kv.shape, bf),
            pltpu.VMEM(span_kv.shape, bf),
            pltpu.VMEM((n * per, rows, width), bf),
            pltpu.VMEM((n * per, rows, width), bf),
            pltpu.VMEM((n, cap_pad, 128), jnp.int32),
            pltpu.VMEM((n, cap_pad, 128), jnp.int32),
            pltpu.VMEM((n * per, rows, width), bf),
            pltpu.VMEM((n * per, rows, width), bf),
            pltpu.VMEM((n, rows, 128), jnp.float32),
            pltpu.VMEM((n, rows, 128), jnp.float32),
            pltpu.VMEM((spans + 1, rows, width), jnp.float32),
            pltpu.VMEM((spans + 1, rows, 128), jnp.float32),
            pltpu.VMEM((spans + 1, rows, 128), jnp.float32),
            pltpu.VMEM((8, blocks * block_len), jnp.int32),
            pltpu.VMEM((rows, width), bf),
            pltpu.VMEM((rows, width), jnp.float32),
            pltpu.VMEM((2, rows, kv_width), jnp.float32),
        ]
        + [pltpu.SemaphoreType.DMA((n,))] * 8
        + [pltpu.SemaphoreType.DMA((2 * heads + 2,))],
        compiler_params=pltpu.CompilerParams(
            collective_id=0, has_side_effects=True, vmem_limit_bytes=56 * 2**20
        ),
        cost_estimate=pl.CostEstimate(
            flops=4 * (spans + cap) * rows * width * blocks * block_len,
            bytes_accessed=12 * 2**20,
            transcendentals=(spans + cap) * rows * heads * sharing * blocks * block_len,
        ),
    )(
        span_dest, span_offset, span_length, seq_length, block_target,
        span_q, span_kv, prefix_kv, resident_kv, decode_q, decode_kv,
    )
    return prefill_out, decode_out


def solution(mesh):
    return jax.shard_map(
        on_device,
        mesh=mesh,
        in_specs=(
            P(("groups", "pool"), None, "tp"),
            P(("groups", "pool"), None, None, "tp"),
            P(("groups", "pool")),
            P(("groups", "pool")),
            P(("groups", "pool")),
            P(("groups", "pool"), None, None, "tp"),
            P(("groups", "pool"), None, None, "tp"),
            P(("groups", "pool")),
            P(("groups", "pool"), None, "tp"),
            P(("groups", "pool"), None, None, "tp"),
            P(("groups", "pool")),
        ),
        out_specs=(P(("groups", "pool"), None, "tp"), P(("groups", "pool"), None, "tp")),
        check_vma=False,
    )
```

```python
import functools

import jax
import jax.numpy as jnp
from jax import lax
from jax.experimental import pallas as pl
from jax.experimental.pallas import tpu as pltpu
from jax.sharding import PartitionSpec as P

HD = 128
SCALE = HD ** (-0.5)
LOW = -1e30
NT = (((1,), (1,)), ((), ()))
NN = (((1,), (0,)), ((), ()))


def soft(scores):
    top = jnp.max(scores, axis=-1, keepdims=True)
    weights = jnp.exp((scores - top) * SCALE)
    return top, weights.astype(jnp.bfloat16), jnp.sum(weights, axis=-1, keepdims=True)


def kernel(
    n, cap, rows, heads, sharing, steps,
    dest_ref, offset_ref, length_ref, seqlen_ref, target_ref,
    span_q, span_kv, prefix, resident, step_q, step_kv,
    prefill_out, decode_out,
    keys, values, res, own_kv, q_send, q_recv, m_send, m_recv, r_send, r_recv,
    t_send, t_recv, self_acc, self_top, self_total, target_row, decode_q, decode_pair, new_kv,
    q_ssem, q_rsem, m_ssem, m_rsem, r_ssem, r_rsem, t_ssem, t_rsem, loc_sem,
):
    me = lax.axis_index("pool")
    spans = span_q.shape[0]
    seqs = resident.shape[0]
    per = cap + 1
    width = heads * sharing * HD
    tall = sharing * rows
    count = heads * sharing
    block_len = prefix.shape[2]

    def at(step):
        return lax.rem(me + step, n)

    loads = []
    for k in range(heads):
        cols = pl.ds(k * HD, HD)
        loads.append(pltpu.make_async_copy(prefix.at[:, 0, :, cols], keys.at[k], loc_sem.at[2 * k]))
        loads.append(pltpu.make_async_copy(prefix.at[:, 1, :, cols], values.at[k], loc_sem.at[2 * k + 1]))
    own_load = pltpu.make_async_copy(span_kv, own_kv, loc_sem.at[2 * heads])
    res_load = pltpu.make_async_copy(resident, res, loc_sem.at[2 * heads + 1])
    for load in loads:
        load.start()
    own_load.start()
    res_load.start()

    barrier = pltpu.get_barrier_semaphore()

    @pl.loop(1, n)
    def _(d):
        pl.semaphore_signal(barrier, inc=1, device_id={"pool": at(d)}, device_id_type=pl.DeviceIdType.MESH)

    def shift_of(j):
        away = dest_ref[j] - me
        return jnp.where(away < 0, away + n, away)

    def span_at(d, r):
        pick = seen = jnp.int32(0)
        for j in range(spans):
            hit = shift_of(j) == d
            pick = jnp.where(hit & (seen == r), j, pick)
            seen = seen + hit.astype(jnp.int32)
        return pick

    def rank_of(j):
        rank = jnp.int32(0)
        for i in range(spans):
            rank = rank + ((dest_ref[i] == dest_ref[j]) & (i < j)).astype(jnp.int32)
        return jnp.minimum(rank, cap - 1)

    def fill(buf, meta, d, send):
        @pl.loop(0, cap)
        def _(r):
            pick = span_at(d, r)
            buf[d * per + r] = span_q[pick]
            meta[d, pl.ds(r, 1), :] = jnp.full((1, 128), offset_ref[pick], jnp.int32)
            if send:
                q_copy(d, r, at(d)).start()

        buf[d * per + cap] = decode_q[...]
        if send:
            m_copy(d, at(d)).start()
            q_copy(d, cap, at(d)).start()

    def q_copy(d, r, to):
        return pltpu.make_async_remote_copy(
            src_ref=q_send.at[d * per + r],
            dst_ref=q_recv.at[d * per + r],
            send_sem=q_ssem.at[d * per + r], recv_sem=q_rsem.at[d * per + r],
            device_id={"pool": to}, device_id_type=pl.DeviceIdType.MESH,
        )

    def m_copy(d, to):
        return pltpu.make_async_remote_copy(
            src_ref=m_send.at[d], dst_ref=m_recv.at[d],
            send_sem=m_ssem.at[d], recv_sem=m_rsem.at[d],
            device_id={"pool": to}, device_id_type=pl.DeviceIdType.MESH,
        )

    def t_copy(d, to):
        return pltpu.make_async_remote_copy(
            src_ref=t_send.at[d], dst_ref=t_recv.at[d],
            send_sem=t_ssem.at[d], recv_sem=t_rsem.at[d],
            device_id={"pool": to}, device_id_type=pl.DeviceIdType.MESH,
        )

    def near(i):
        odd = lax.rem(i, 2)
        return odd * ((i + 1) // 2) + (1 - odd) * (n - i // 2)

    def r_copy(d, r, to):
        return pltpu.make_async_remote_copy(
            src_ref=r_send.at[d * per + r],
            dst_ref=r_recv.at[d * per + r],
            send_sem=r_ssem.at[d * per + r], recv_sem=r_rsem.at[d * per + r],
            device_id={"pool": to}, device_id_type=pl.DeviceIdType.MESH,
        )

    for s in range(seqs):
        part = slice(s * steps, (s + 1) * steps)
        decode_pair[part, :] = step_q[s].astype(jnp.float32)
        for k in range(2):
            new_kv[k, part, :] = step_kv[s, k].astype(jnp.float32)
    decode_q[...] = decode_pair[...].astype(jnp.bfloat16)
    m_send[...] = jnp.zeros_like(m_send)
    m_recv[0] = jnp.zeros(m_recv.shape[1:], jnp.int32)
    pl.semaphore_wait(barrier, n - 1)

    @pl.loop(1, n)
    def _(i):
        d = near(i)
        fill(q_send, m_send, d, True)

    fill(q_recv, m_recv, 0, False)
    for b in range(prefix.shape[0]):
        target_row[:, b * block_len : (b + 1) * block_len] = jnp.full((8, block_len), target_ref[b], jnp.int32)

    lane = lax.broadcasted_iota(jnp.int32, (rows, 128), 1)

    def stacked(block, k):
        base = k * sharing * HD
        return jnp.concatenate(
            [block[:, base + g * HD : base + (g + 1) * HD] for g in range(sharing)], axis=0
        )

    def spread(tops, totals, top, total, k):
        for g in range(sharing):
            h = k * sharing + g
            part = slice(g * rows, (g + 1) * rows)
            tops = jnp.where(lane == h, top[part], tops)
            totals = jnp.where(lane == h, total[part], totals)
        return tops, totals

    def attend(buf, out, stats, d, r, bias):
        slot = d * per + r
        block = buf[slot]
        tile = stats[d]
        for k in range(heads):
            query = stacked(block, k)
            key = keys[k].reshape(-1, HD)
            value = values[k].reshape(-1, HD)
            score = lax.dot_general(query, key, NT, preferred_element_type=jnp.float32)
            if bias.shape[0] == 1:
                score = score + bias
            else:
                score = (score.reshape(sharing, rows, -1) + bias[None]).reshape(tall, -1)
            top, weight, total = soft(score)
            acc = lax.dot_general(weight, value, NN, preferred_element_type=jnp.float32)
            for g in range(sharing):
                h = k * sharing + g
                out[slot, :, h * HD : (h + 1) * HD] = acc[g * rows : (g + 1) * rows].astype(jnp.bfloat16)
            for g in range(sharing):
                part = slice(g * rows, (g + 1) * rows)
                spot = r * 2 * count + k * sharing + g
                tile = jnp.where(lane == spot, top[part], tile)
                tile = jnp.where(lane == spot + count, total[part], tile)
        stats[d] = tile

    tokens = keys.shape[1] * keys.shape[2]
    position = lax.broadcasted_iota(jnp.int32, (1, tokens), 1)

    def chunk(out, stats, d, away):
        source = lax.rem(me - d + n, n)
        stats[d] = jnp.zeros((rows, 128), jnp.float32)

        @pl.loop(0, cap)
        def _(r):
            if away:
                q_copy(d, r, at(d)).wait_recv()
            limit = m_recv[d, pl.ds(r, 1), :][:, :1]
            attend(q_recv, out, stats, d, r, jnp.where(position < limit, 0.0, LOW))
            if away:
                r_copy(d, r, source).start()

        if away:
            q_copy(d, cap, at(d)).wait_recv()
        seq = source * seqs + lax.broadcasted_iota(jnp.int32, (rows, 1), 0) // steps
        attend(q_recv, out, stats, d, cap, jnp.where(target_row[0:1, :] == seq, 0.0, LOW))
        if away:
            r_copy(d, cap, source).start()
            t_copy(d, source).start()

    for load in loads:
        load.wait()
    chunk(r_recv, t_recv, 0, False)

    @pl.loop(1, n)
    def _(i):
        d = near(i)
        m_copy(d, at(d)).wait_recv()
        chunk(r_send, t_send, d, True)

    own_load.wait()
    row_of = lax.rem(lax.broadcasted_iota(jnp.int32, (tall, rows), 0), rows)
    col_of = lax.broadcasted_iota(jnp.int32, (tall, rows), 1)

    def keep(index, k, acc, tops, totals, top, total):
        for g in range(sharing):
            h = k * sharing + g
            self_acc[index, :, h * HD : (h + 1) * HD] = acc[g * rows : (g + 1) * rows]
        return spread(tops, totals, top, total, k)

    @pl.loop(0, spans)
    def _(j):
        block = span_q[j]
        tops = totals = jnp.zeros((rows, 128), jnp.float32)
        for k in range(heads):
            cols = slice(k * HD, (k + 1) * HD)
            score = lax.dot_general(
                stacked(block, k), own_kv[j, 0, :, cols], NT, preferred_element_type=jnp.float32
            )
            top, weight, total = soft(jnp.where(col_of <= row_of, score, LOW))
            acc = lax.dot_general(weight, own_kv[j, 1, :, cols], NN, preferred_element_type=jnp.float32)
            tops, totals = keep(j, k, acc, tops, totals, top, total)
        self_top[j] = tops
        self_total[j] = totals

    res_load.wait()
    res_len = resident.shape[2]
    slot_of = lax.broadcasted_iota(jnp.int32, (1, res_len), 1)
    row_seq = lax.rem(lax.broadcasted_iota(jnp.int32, (tall, 1), 0), rows) // steps
    tops = totals = jnp.zeros((rows, 128), jnp.float32)
    for k in range(heads):
        cols = slice(k * HD, (k + 1) * HD)
        query = stacked(decode_q[...], k)

        def one(s, carry):
            acc, top, total = carry
            score = lax.dot_general(query, res[s, 0, :, cols], NT, preferred_element_type=jnp.float32)
            score = score + jnp.where(slot_of < seqlen_ref[s], 0.0, LOW)
            top_s, weight, total_s = soft(score)
            acc_s = lax.dot_general(weight, res[s, 1, :, cols], NN, preferred_element_type=jnp.float32)
            here = row_seq == s
            return jnp.where(here, acc_s, acc), jnp.where(here, top_s, top), jnp.where(here, total_s, total)

        zero = jnp.zeros((tall, 1), jnp.float32)
        acc, top, total = lax.fori_loop(0, seqs, one, (jnp.zeros((tall, HD), jnp.float32), zero, zero))
        score = lax.dot_general(query, new_kv[0, :, cols].astype(jnp.bfloat16), NT, preferred_element_type=jnp.float32)
        fits = (col_of // steps == row_of // steps) & (col_of <= row_of)
        top_n, weight, total_n = soft(jnp.where(fits, score, LOW))
        acc_n = lax.dot_general(weight, new_kv[1, :, cols].astype(jnp.bfloat16), NN, preferred_element_type=jnp.float32)
        best = jnp.maximum(top, top_n)
        a = jnp.exp((top - best) * SCALE)
        b = jnp.exp((top_n - best) * SCALE)
        tops, totals = keep(spans, k, acc * a + acc_n * b, tops, totals, best, total * a + total_n * b)
    self_top[spans] = tops
    self_total[spans] = totals

    @pl.loop(1, n)
    def _(d):
        source = lax.rem(me - d + n, n)
        m_copy(d, at(d)).wait_send()
        t_copy(d, source).wait_recv()

        @pl.loop(0, per)
        def _(r):
            q_copy(d, r, at(d)).wait_send()
            r_copy(d, r, source).wait_recv()

    def stats_of(tile, rank):
        top = tile
        for r in range(1, per):
            top = jnp.where(rank == r, pltpu.roll(tile, 128 - r * 2 * count, 1), top)
        return top, pltpu.roll(top, 128 - count, 1)

    live_row = lax.broadcasted_iota(jnp.int32, (rows, 128), 0)

    @pl.loop(0, spans)
    def _(j):
        away = shift_of(j)
        rank = rank_of(j)
        got = r_recv[away * per + rank]
        top, total = stats_of(t_recv[away], rank)
        own = self_top[j]
        best = jnp.maximum(top, own)
        a = jnp.exp((top - best) * SCALE)
        b = jnp.exp((own - best) * SCALE)
        share = total * a + self_total[j] * b
        live = live_row < length_ref[j]
        share = jnp.where(lane < count, share, 1.0)
        a = jnp.where(live, a / share, 0.0)
        b = jnp.where(live, b / share, 0.0)
        for h in range(heads * sharing):
            cols = slice(h * HD, (h + 1) * HD)
            out = got[:, cols].astype(jnp.float32) * a[:, h : h + 1] + self_acc[j, :, cols] * b[:, h : h + 1]
            prefill_out[j, :, cols] = out.astype(jnp.bfloat16)

    @pl.loop(0, n)
    def _(d):
        got = r_recv[d * per + cap]
        top, total = stats_of(t_recv[d], cap)
        own = self_top[spans]
        best = jnp.maximum(top, own)
        a = jnp.exp((top - best) * SCALE)
        b = jnp.exp((own - best) * SCALE)
        for h in range(heads * sharing):
            cols = slice(h * HD, (h + 1) * HD)
            self_acc[spans, :, cols] = (
                got[:, cols].astype(jnp.float32) * a[:, h : h + 1]
                + self_acc[spans, :, cols] * b[:, h : h + 1]
            )
        self_total[spans] = total * a + self_total[spans] * b
        self_top[spans] = best

    share = self_total[spans]
    for h in range(count):
        cols = slice(h * HD, (h + 1) * HD)
        decode_pair[:, cols] = self_acc[spans, :, cols] / share[:, h : h + 1]
    for s in range(seqs):
        decode_out[s] = decode_pair[s * steps : (s + 1) * steps, :].astype(jnp.bfloat16)

    @pl.loop(1, n)
    def _(d):
        t_copy(d, lax.rem(me - d + n, n)).wait_send()

        @pl.loop(0, per)
        def _(r):
            r_copy(d, r, lax.rem(me - d + n, n)).wait_send()


def on_device(
    span_q, span_kv, span_offset, span_length, span_dest, prefix_kv,
    resident_kv, seq_length, decode_q, decode_kv, block_target,
):
    n = lax.axis_size("pool")
    spans, rows, width = span_q.shape
    kv_width = span_kv.shape[-1]
    heads = kv_width // HD
    sharing = width // kv_width
    seqs, steps = decode_q.shape[:2]
    blocks, _, block_len, _ = prefix_kv.shape
    cap = -(-spans // n)
    per = cap + 1
    cap_pad = -(-cap // 8) * 8

    bf = jnp.bfloat16
    smem = pl.BlockSpec(memory_space=pltpu.SMEM)
    vmem = pl.BlockSpec(memory_space=pltpu.VMEM)
    hbm = pl.BlockSpec(memory_space=pl.ANY)
    prefill_out, decode_out = pl.pallas_call(
        functools.partial(kernel, n, cap, rows, heads, sharing, steps),
        out_shape=(
            jax.ShapeDtypeStruct((spans, rows, width), bf),
            jax.ShapeDtypeStruct((seqs, steps, width), bf),
        ),
        in_specs=[smem] * 5 + [vmem, hbm, hbm, hbm, vmem, vmem],
        out_specs=(vmem, vmem),
        scratch_shapes=[
            pltpu.VMEM((heads, blocks, block_len, HD), bf),
            pltpu.VMEM((heads, blocks, block_len, HD), bf),
            pltpu.VMEM(resident_kv.shape, bf),
            pltpu.VMEM(span_kv.shape, bf),
            pltpu.VMEM((n * per, rows, width), bf),
            pltpu.VMEM((n * per, rows, width), bf),
            pltpu.VMEM((n, cap_pad, 128), jnp.int32),
            pltpu.VMEM((n, cap_pad, 128), jnp.int32),
            pltpu.VMEM((n * per, rows, width), bf),
            pltpu.VMEM((n * per, rows, width), bf),
            pltpu.VMEM((n, rows, 128), jnp.float32),
            pltpu.VMEM((n, rows, 128), jnp.float32),
            pltpu.VMEM((spans + 1, rows, width), jnp.float32),
            pltpu.VMEM((spans + 1, rows, 128), jnp.float32),
            pltpu.VMEM((spans + 1, rows, 128), jnp.float32),
            pltpu.VMEM((8, blocks * block_len), jnp.int32),
            pltpu.VMEM((rows, width), bf),
            pltpu.VMEM((rows, width), jnp.float32),
            pltpu.VMEM((2, rows, kv_width), jnp.float32),
        ]
        + [pltpu.SemaphoreType.DMA((n * per,))] * 2
        + [pltpu.SemaphoreType.DMA((n,))] * 2
        + [pltpu.SemaphoreType.DMA((n * per,))] * 2
        + [pltpu.SemaphoreType.DMA((n,))] * 2
        + [pltpu.SemaphoreType.DMA((2 * heads + 2,))],
        compiler_params=pltpu.CompilerParams(
            collective_id=0, has_side_effects=True, vmem_limit_bytes=56 * 2**20
        ),
        cost_estimate=pl.CostEstimate(
            flops=4 * (spans + cap) * rows * width * blocks * block_len,
            bytes_accessed=12 * 2**20,
            transcendentals=(spans + cap) * rows * heads * sharing * blocks * block_len,
        ),
    )(
        span_dest, span_offset, span_length, seq_length, block_target,
        span_q, span_kv, prefix_kv, resident_kv, decode_q, decode_kv,
    )
    return prefill_out, decode_out


def solution(mesh):
    return jax.shard_map(
        on_device,
        mesh=mesh,
        in_specs=(
            P(("groups", "pool"), None, "tp"),
            P(("groups", "pool"), None, None, "tp"),
            P(("groups", "pool")),
            P(("groups", "pool")),
            P(("groups", "pool")),
            P(("groups", "pool"), None, None, "tp"),
            P(("groups", "pool"), None, None, "tp"),
            P(("groups", "pool")),
            P(("groups", "pool"), None, "tp"),
            P(("groups", "pool"), None, None, "tp"),
            P(("groups", "pool")),
        ),
        out_specs=(P(("groups", "pool"), None, "tp"), P(("groups", "pool"), None, "tp")),
        check_vma=False,
    )
```

```python
import functools

import jax
import jax.numpy as jnp
from jax import lax
from jax.experimental import pallas as pl
from jax.experimental.pallas import tpu as pltpu
from jax.sharding import PartitionSpec as P

HD = 128
SCALE = HD ** (-0.5)
LOW = -1e30
NT = (((1,), (1,)), ((), ()))
NN = (((1,), (0,)), ((), ()))


def soft(scores):
    top = jnp.max(scores, axis=-1, keepdims=True)
    weights = jnp.exp((scores - top) * SCALE)
    return top, weights.astype(jnp.bfloat16), jnp.sum(weights, axis=-1, keepdims=True)


def kernel(
    n, cap, rows, heads, sharing, steps,
    dest_ref, offset_ref, length_ref, seqlen_ref, target_ref,
    span_q, span_kv, prefix, resident, step_q, step_kv,
    prefill_out, decode_out,
    keys, values, res, own_kv, q_send, q_recv, m_send, m_recv, r_send, r_recv,
    t_send, t_recv, self_acc, self_top, self_total, target_row, decode_q, decode_pair, new_kv,
    q_ssem, q_rsem, m_ssem, m_rsem, r_ssem, r_rsem, t_ssem, t_rsem, loc_sem,
):
    me = lax.axis_index("pool")
    spans = span_q.shape[0]
    seqs = resident.shape[0]
    per = cap + 1
    width = heads * sharing * HD
    tall = sharing * rows
    count = heads * sharing
    block_len = prefix.shape[2]

    def at(step):
        return lax.rem(me + step, n)

    loads = []
    for k in range(heads):
        cols = pl.ds(k * HD, HD)
        loads.append(pltpu.make_async_copy(prefix.at[:, 0, :, cols], keys.at[k], loc_sem.at[2 * k]))
        loads.append(pltpu.make_async_copy(prefix.at[:, 1, :, cols], values.at[k], loc_sem.at[2 * k + 1]))
    own_load = pltpu.make_async_copy(span_kv, own_kv, loc_sem.at[2 * heads])
    res_load = pltpu.make_async_copy(resident, res, loc_sem.at[2 * heads + 1])
    for load in loads:
        load.start()
    own_load.start()
    res_load.start()

    barrier = pltpu.get_barrier_semaphore()

    @pl.loop(1, n)
    def _(d):
        pl.semaphore_signal(barrier, inc=1, device_id={"pool": at(d)}, device_id_type=pl.DeviceIdType.MESH)

    def shift_of(j):
        away = dest_ref[j] - me
        return jnp.where(away < 0, away + n, away)

    def span_at(d, r):
        pick = seen = jnp.int32(0)
        for j in range(spans):
            hit = shift_of(j) == d
            pick = jnp.where(hit & (seen == r), j, pick)
            seen = seen + hit.astype(jnp.int32)
        return pick

    def rank_of(j):
        rank = jnp.int32(0)
        for i in range(spans):
            rank = rank + ((dest_ref[i] == dest_ref[j]) & (i < j)).astype(jnp.int32)
        return jnp.minimum(rank, cap - 1)

    def fill(buf, meta, d, send):
        @pl.loop(0, cap)
        def _(r):
            pick = span_at(d, r)
            buf[d * per + r] = span_q[pick]
            meta[d, pl.ds(r, 1), :] = jnp.full((1, 128), offset_ref[pick], jnp.int32)
            if send:
                q_copy(d, r, at(d)).start()

        buf[d * per + cap] = decode_q[...]
        if send:
            m_copy(d, at(d)).start()
            q_copy(d, cap, at(d)).start()

    def q_copy(d, r, to):
        return pltpu.make_async_remote_copy(
            src_ref=q_send.at[d * per + r],
            dst_ref=q_recv.at[d * per + r],
            send_sem=q_ssem.at[d * per + r], recv_sem=q_rsem.at[d * per + r],
            device_id={"pool": to}, device_id_type=pl.DeviceIdType.MESH,
        )

    def m_copy(d, to):
        return pltpu.make_async_remote_copy(
            src_ref=m_send.at[d], dst_ref=m_recv.at[d],
            send_sem=m_ssem.at[d], recv_sem=m_rsem.at[d],
            device_id={"pool": to}, device_id_type=pl.DeviceIdType.MESH,
        )

    def t_copy(d, to):
        return pltpu.make_async_remote_copy(
            src_ref=t_send.at[d], dst_ref=t_recv.at[d],
            send_sem=t_ssem.at[d], recv_sem=t_rsem.at[d],
            device_id={"pool": to}, device_id_type=pl.DeviceIdType.MESH,
        )

    def near(i):
        odd = lax.rem(i, 2)
        return odd * ((i + 1) // 2) + (1 - odd) * (n - i // 2)

    def r_copy(d, r, to):
        return pltpu.make_async_remote_copy(
            src_ref=r_send.at[d * per + r],
            dst_ref=r_recv.at[d * per + r],
            send_sem=r_ssem.at[d * per + r], recv_sem=r_rsem.at[d * per + r],
            device_id={"pool": to}, device_id_type=pl.DeviceIdType.MESH,
        )

    for s in range(seqs):
        part = slice(s * steps, (s + 1) * steps)
        decode_pair[part, :] = step_q[s].astype(jnp.float32)
        for k in range(2):
            new_kv[k, part, :] = step_kv[s, k].astype(jnp.float32)
    decode_q[...] = decode_pair[...].astype(jnp.bfloat16)
    m_send[...] = jnp.zeros_like(m_send)
    m_recv[0] = jnp.zeros(m_recv.shape[1:], jnp.int32)
    pl.semaphore_wait(barrier, n - 1)

    @pl.loop(1, n)
    def _(i):
        d = near(i)
        fill(q_send, m_send, d, True)

    fill(q_recv, m_recv, 0, False)
    for b in range(prefix.shape[0]):
        target_row[:, b * block_len : (b + 1) * block_len] = jnp.full((8, block_len), target_ref[b], jnp.int32)

    lane = lax.broadcasted_iota(jnp.int32, (rows, 128), 1)

    def stacked(block, k):
        base = k * sharing * HD
        return jnp.concatenate(
            [block[:, base + g * HD : base + (g + 1) * HD] for g in range(sharing)], axis=0
        )

    def spread(tops, totals, top, total, k):
        for g in range(sharing):
            h = k * sharing + g
            part = slice(g * rows, (g + 1) * rows)
            tops = jnp.where(lane == h, top[part], tops)
            totals = jnp.where(lane == h, total[part], totals)
        return tops, totals

    def attend(buf, out, stats, d, r, bias):
        slot = d * per + r
        block = buf[slot]
        tile = stats[d]
        for k in range(heads):
            query = stacked(block, k)
            key = keys[k].reshape(-1, HD)
            value = values[k].reshape(-1, HD)
            score = lax.dot_general(query, key, NT, preferred_element_type=jnp.float32)
            if bias.shape[0] == 1:
                score = score + bias
            else:
                score = (score.reshape(sharing, rows, -1) + bias[None]).reshape(tall, -1)
            top, weight, total = soft(score)
            acc = lax.dot_general(weight, value, NN, preferred_element_type=jnp.float32)
            for g in range(sharing):
                h = k * sharing + g
                out[slot, :, h * HD : (h + 1) * HD] = acc[g * rows : (g + 1) * rows].astype(jnp.bfloat16)
            for g in range(sharing):
                part = slice(g * rows, (g + 1) * rows)
                spot = r * 2 * count + k * sharing + g
                tile = jnp.where(lane == spot, top[part], tile)
                tile = jnp.where(lane == spot + count, total[part], tile)
        stats[d] = tile

    tokens = keys.shape[1] * keys.shape[2]
    position = lax.broadcasted_iota(jnp.int32, (1, tokens), 1)

    def chunk(out, stats, d, away):
        source = lax.rem(me - d + n, n)
        stats[d] = jnp.zeros((rows, 128), jnp.float32)

        @pl.loop(0, cap)
        def _(r):
            if away:
                q_copy(d, r, at(d)).wait_recv()
            limit = m_recv[d, pl.ds(r, 1), :][:, :1]
            attend(q_recv, out, stats, d, r, jnp.where(position < limit, 0.0, LOW))
            if away:
                r_copy(d, r, source).start()

        if away:
            q_copy(d, cap, at(d)).wait_recv()
        seq = source * seqs + lax.broadcasted_iota(jnp.int32, (rows, 1), 0) // steps
        attend(q_recv, out, stats, d, cap, jnp.where(target_row[0:1, :] == seq, 0.0, LOW))
        if away:
            r_copy(d, cap, source).start()
            t_copy(d, source).start()

    for load in loads:
        load.wait()
    chunk(r_recv, t_recv, 0, False)

    @pl.loop(1, n)
    def _(i):
        d = near(i)
        m_copy(d, at(d)).wait_recv()
        chunk(r_send, t_send, d, True)

    own_load.wait()
    row_of = lax.rem(lax.broadcasted_iota(jnp.int32, (tall, rows), 0), rows)
    col_of = lax.broadcasted_iota(jnp.int32, (tall, rows), 1)

    def keep(index, k, acc, tops, totals, top, total):
        for g in range(sharing):
            h = k * sharing + g
            self_acc[index, :, h * HD : (h + 1) * HD] = acc[g * rows : (g + 1) * rows]
        return spread(tops, totals, top, total, k)

    @pl.loop(0, spans)
    def _(j):
        block = span_q[j]
        tops = totals = jnp.zeros((rows, 128), jnp.float32)
        for k in range(heads):
            cols = slice(k * HD, (k + 1) * HD)
            score = lax.dot_general(
                stacked(block, k), own_kv[j, 0, :, cols], NT, preferred_element_type=jnp.float32
            )
            top, weight, total = soft(jnp.where(col_of <= row_of, score, LOW))
            acc = lax.dot_general(weight, own_kv[j, 1, :, cols], NN, preferred_element_type=jnp.float32)
            tops, totals = keep(j, k, acc, tops, totals, top, total)
        self_top[j] = tops
        self_total[j] = totals

    res_load.wait()
    res_len = resident.shape[2]
    slot_of = lax.broadcasted_iota(jnp.int32, (1, res_len), 1)
    row_seq = lax.rem(lax.broadcasted_iota(jnp.int32, (tall, 1), 0), rows) // steps
    tops = totals = jnp.zeros((rows, 128), jnp.float32)
    for k in range(heads):
        cols = slice(k * HD, (k + 1) * HD)
        query = stacked(decode_q[...], k)

        def one(s, carry):
            acc, top, total = carry
            score = lax.dot_general(query, res[s, 0, :, cols], NT, preferred_element_type=jnp.float32)
            score = score + jnp.where(slot_of < seqlen_ref[s], 0.0, LOW)
            top_s, weight, total_s = soft(score)
            acc_s = lax.dot_general(weight, res[s, 1, :, cols], NN, preferred_element_type=jnp.float32)
            here = row_seq == s
            return jnp.where(here, acc_s, acc), jnp.where(here, top_s, top), jnp.where(here, total_s, total)

        zero = jnp.zeros((tall, 1), jnp.float32)
        acc, top, total = lax.fori_loop(0, seqs, one, (jnp.zeros((tall, HD), jnp.float32), zero, zero))
        score = lax.dot_general(query, new_kv[0, :, cols].astype(jnp.bfloat16), NT, preferred_element_type=jnp.float32)
        fits = (col_of // steps == row_of // steps) & (col_of <= row_of)
        top_n, weight, total_n = soft(jnp.where(fits, score, LOW))
        acc_n = lax.dot_general(weight, new_kv[1, :, cols].astype(jnp.bfloat16), NN, preferred_element_type=jnp.float32)
        best = jnp.maximum(top, top_n)
        a = jnp.exp((top - best) * SCALE)
        b = jnp.exp((top_n - best) * SCALE)
        tops, totals = keep(spans, k, acc * a + acc_n * b, tops, totals, best, total * a + total_n * b)
    self_top[spans] = tops
    self_total[spans] = totals

    def stats_of(tile, rank):
        top = tile
        for r in range(1, per):
            top = jnp.where(rank == r, pltpu.roll(tile, 128 - r * 2 * count, 1), top)
        return top, pltpu.roll(top, 128 - count, 1)

    def merge_decode(d):
        got = r_recv[d * per + cap]
        top, total = stats_of(t_recv[d], cap)
        own = self_top[spans]
        best = jnp.maximum(top, own)
        a = jnp.exp((top - best) * SCALE)
        b = jnp.exp((own - best) * SCALE)
        for h in range(heads * sharing):
            cols = slice(h * HD, (h + 1) * HD)
            self_acc[spans, :, cols] = (
                got[:, cols].astype(jnp.float32) * a[:, h : h + 1]
                + self_acc[spans, :, cols] * b[:, h : h + 1]
            )
        self_total[spans] = total * a + self_total[spans] * b
        self_top[spans] = best

    merge_decode(0)

    @pl.loop(1, n)
    def _(i):
        d = near(i)
        source = lax.rem(me - d + n, n)
        m_copy(d, at(d)).wait_send()
        t_copy(d, source).wait_recv()

        @pl.loop(0, per)
        def _(r):
            q_copy(d, r, at(d)).wait_send()
            r_copy(d, r, source).wait_recv()

        merge_decode(d)

    live_row = lax.broadcasted_iota(jnp.int32, (rows, 128), 0)

    @pl.loop(0, spans)
    def _(j):
        away = shift_of(j)
        rank = rank_of(j)
        got = r_recv[away * per + rank]
        top, total = stats_of(t_recv[away], rank)
        own = self_top[j]
        best = jnp.maximum(top, own)
        a = jnp.exp((top - best) * SCALE)
        b = jnp.exp((own - best) * SCALE)
        share = total * a + self_total[j] * b
        live = live_row < length_ref[j]
        share = jnp.where(lane < count, share, 1.0)
        a = jnp.where(live, a / share, 0.0)
        b = jnp.where(live, b / share, 0.0)
        for h in range(heads * sharing):
            cols = slice(h * HD, (h + 1) * HD)
            out = got[:, cols].astype(jnp.float32) * a[:, h : h + 1] + self_acc[j, :, cols] * b[:, h : h + 1]
            prefill_out[j, :, cols] = out.astype(jnp.bfloat16)

    share = self_total[spans]
    for h in range(count):
        cols = slice(h * HD, (h + 1) * HD)
        decode_pair[:, cols] = self_acc[spans, :, cols] / share[:, h : h + 1]
    for s in range(seqs):
        decode_out[s] = decode_pair[s * steps : (s + 1) * steps, :].astype(jnp.bfloat16)

    @pl.loop(1, n)
    def _(d):
        t_copy(d, lax.rem(me - d + n, n)).wait_send()

        @pl.loop(0, per)
        def _(r):
            r_copy(d, r, lax.rem(me - d + n, n)).wait_send()


def on_device(
    span_q, span_kv, span_offset, span_length, span_dest, prefix_kv,
    resident_kv, seq_length, decode_q, decode_kv, block_target,
):
    n = lax.axis_size("pool")
    spans, rows, width = span_q.shape
    kv_width = span_kv.shape[-1]
    heads = kv_width // HD
    sharing = width // kv_width
    seqs, steps = decode_q.shape[:2]
    blocks, _, block_len, _ = prefix_kv.shape
    cap = -(-spans // n)
    per = cap + 1
    cap_pad = -(-cap // 8) * 8

    bf = jnp.bfloat16
    smem = pl.BlockSpec(memory_space=pltpu.SMEM)
    vmem = pl.BlockSpec(memory_space=pltpu.VMEM)
    hbm = pl.BlockSpec(memory_space=pl.ANY)
    prefill_out, decode_out = pl.pallas_call(
        functools.partial(kernel, n, cap, rows, heads, sharing, steps),
        out_shape=(
            jax.ShapeDtypeStruct((spans, rows, width), bf),
            jax.ShapeDtypeStruct((seqs, steps, width), bf),
        ),
        in_specs=[smem] * 5 + [vmem, hbm, hbm, hbm, vmem, vmem],
        out_specs=(vmem, vmem),
        scratch_shapes=[
            pltpu.VMEM((heads, blocks, block_len, HD), bf),
            pltpu.VMEM((heads, blocks, block_len, HD), bf),
            pltpu.VMEM(resident_kv.shape, bf),
            pltpu.VMEM(span_kv.shape, bf),
            pltpu.VMEM((n * per, rows, width), bf),
            pltpu.VMEM((n * per, rows, width), bf),
            pltpu.VMEM((n, cap_pad, 128), jnp.int32),
            pltpu.VMEM((n, cap_pad, 128), jnp.int32),
            pltpu.VMEM((n * per, rows, width), bf),
            pltpu.VMEM((n * per, rows, width), bf),
            pltpu.VMEM((n, rows, 128), jnp.float32),
            pltpu.VMEM((n, rows, 128), jnp.float32),
            pltpu.VMEM((spans + 1, rows, width), jnp.float32),
            pltpu.VMEM((spans + 1, rows, 128), jnp.float32),
            pltpu.VMEM((spans + 1, rows, 128), jnp.float32),
            pltpu.VMEM((8, blocks * block_len), jnp.int32),
            pltpu.VMEM((rows, width), bf),
            pltpu.VMEM((rows, width), jnp.float32),
            pltpu.VMEM((2, rows, kv_width), jnp.float32),
        ]
        + [pltpu.SemaphoreType.DMA((n * per,))] * 2
        + [pltpu.SemaphoreType.DMA((n,))] * 2
        + [pltpu.SemaphoreType.DMA((n * per,))] * 2
        + [pltpu.SemaphoreType.DMA((n,))] * 2
        + [pltpu.SemaphoreType.DMA((2 * heads + 2,))],
        compiler_params=pltpu.CompilerParams(
            collective_id=0, has_side_effects=True, vmem_limit_bytes=56 * 2**20
        ),
        cost_estimate=pl.CostEstimate(
            flops=4 * (spans + cap) * rows * width * blocks * block_len,
            bytes_accessed=12 * 2**20,
            transcendentals=(spans + cap) * rows * heads * sharing * blocks * block_len,
        ),
    )(
        span_dest, span_offset, span_length, seq_length, block_target,
        span_q, span_kv, prefix_kv, resident_kv, decode_q, decode_kv,
    )
    return prefill_out, decode_out


def solution(mesh):
    return jax.shard_map(
        on_device,
        mesh=mesh,
        in_specs=(
            P(("groups", "pool"), None, "tp"),
            P(("groups", "pool"), None, None, "tp"),
            P(("groups", "pool")),
            P(("groups", "pool")),
            P(("groups", "pool")),
            P(("groups", "pool"), None, None, "tp"),
            P(("groups", "pool"), None, None, "tp"),
            P(("groups", "pool")),
            P(("groups", "pool"), None, "tp"),
            P(("groups", "pool"), None, None, "tp"),
            P(("groups", "pool")),
        ),
        out_specs=(P(("groups", "pool"), None, "tp"), P(("groups", "pool"), None, "tp")),
        check_vma=False,
    )
```
